128 devices in a mesh: tm: 8 (over x, core), seq: 16 (over z, y).
Axes of the slice: x: 4, y: 4, z: 4, core: 2. Of those that a mesh axis runs over, the one named last changes fastest.
Arguments:
- hidden: bfloat16 [8, 2, 2048, 2432], P('tm', None, 'seq'), may hold values from -6 to 6
- text_states: bfloat16 [8, 2, 256, 2560], P('tm', None, 'seq'), may hold values from -6 to 6
- text_lengths: int32 [2], replicated, may hold values from 1 to 256
- plan_index: int32 [8], P('tm'), may hold values from 0 to 27, as said below
- modulation: float32 [8, 5, 2432], P('tm'), may hold values from -3 to 3
- query_key_value_weight: bfloat16 [2432, 3840], replicated, may hold values from -0.125 to 0.125
- query_gain: float32 [64], replicated, may hold values from 0.5 to 7
- key_gain: float32 [64], replicated, may hold values from 0.5 to 7
- attention_output_weight: bfloat16 [1280, 2432], replicated, may hold values from -0.15625 to 0.15625
- latent_output_weight: bfloat16 [2432, 64], replicated, may hold values from -0.125 to 0.125
- anchor: float32 [2048, 64], P('seq'), may hold values from -6 to 6
Outputs:
- velocity: float32 [8, 2048, 64], P('tm', 'seq')
- latents: float32 [8, 2048, 64], P('tm', 'seq')
The draws below stay inside these ranges and needn't reach their ends.
Inputs may be any that keep to these rules, and one draw needn't show every extreme that they name: `plan_index`: strictly increasing along the window; the last window step is at plan position 27.
All inputs are finite; a program needn't handle non-finite values.
Results may differ from the reference program's by a relative error of at most 0.0075.
The reference program's roundings to bfloat16 on the way count: a program that leaves them out, or rounds other values in their place, can miss the bound.
Values may be sent and summed in bfloat16 or wider, within the bound.
A program may use at most 192 MiB of HBM per device.

```python
import math
import jax
import jax.numpy as jnp
from jax import lax

D = 2432
HD = 64
C = 64
NSTEPS = 28
ATT = 1280
WINDOW = 8
IMG = 2048
TXT = 256


def draw_plan_index(key, part):
    key = jax.random.fold_in(key, 11)
    order = jax.random.permutation(key, NSTEPS - 1)
    earlier = jnp.sort(order[:WINDOW - 1]).astype(jnp.int32)
    return jnp.concatenate([earlier, jnp.full((1,), NSTEPS - 1, dtype=jnp.int32)]).astype(jnp.int32)


def spread_gain(key, lower, upper):
    uniform_part = jax.random.uniform(key, (HD,), dtype=jnp.float32)
    return jnp.exp(jnp.log(lower) + uniform_part * (jnp.log(upper) - jnp.log(lower)))


def draw_query_gain(key, part):
    key = jax.random.fold_in(key, 12)
    return spread_gain(key, 0.5, 2.0)


def draw_key_gain(key, part):
    key = jax.random.fold_in(key, 13)
    return spread_gain(key, 0.5, 2.0)


def block_levels(own_key, shape, shards, low, largest):
    level = 1.0
    for dim, blocks in shards:
        steps = jax.random.uniform(jax.random.fold_in(jax.random.fold_in(own_key, 6), dim), (blocks,), jnp.float32, low / len(shards), largest / len(shards))
        level = level * jnp.repeat(jnp.exp(steps), shape[dim] // blocks).reshape((-1,) + (1,) * (len(shape) - 1 - dim))
    return level


def gaussian(rng, extent, scale, limit, cuts=(), held_as=jnp.bfloat16):
    array = scale * jax.random.normal(rng, extent, jnp.float32)
    if cuts:
        array = array * block_levels(rng, extent, cuts, -0.22, 0.18)
    return jnp.clip(array, -limit, limit).astype(held_as)


def setup_inputs(seed: int = 0) -> dict:
    streams_of = jax.random.split(jax.random.key(seed), 12)
    hidden = gaussian(streams_of[0], (WINDOW, 2, IMG, D), 1.0, 6.0, ((0, 8), (2, 16)))
    text_states = gaussian(streams_of[1], (WINDOW, 2, TXT, 2 * ATT), 1.0, 6.0, ((0, 8), (2, 16)))
    text_lengths = jax.random.randint(streams_of[2], (2,), 1, TXT + 1).astype(jnp.int32)
    plan_index = draw_plan_index(jax.random.fold_in(streams_of[11], 71), 0)
    modulation = gaussian(streams_of[4], (WINDOW, 5, D), 0.5, 3.0, ((0, 8),), jnp.float32)
    query_key_value_weight = gaussian(streams_of[5], (D, 3 * ATT), D ** -0.5, 0.125)
    query_gain = draw_query_gain(jax.random.fold_in(streams_of[11], 71), 0)
    key_gain = draw_key_gain(jax.random.fold_in(streams_of[11], 71), 0)
    attention_output_weight = gaussian(streams_of[8], (ATT, D), ATT ** -0.5, 0.15625)
    latent_output_weight = gaussian(streams_of[9], (D, C), D ** -0.5, 0.125)
    anchor = gaussian(streams_of[10], (IMG, C), 1.0, 6.0, ((0, 16),), jnp.float32)
    return {"hidden": hidden, "text_states": text_states, "text_lengths": text_lengths, "plan_index": plan_index, "modulation": modulation, "query_key_value_weight": query_key_value_weight, "query_gain": query_gain, "key_gain": key_gain, "attention_output_weight": attention_output_weight, "latent_output_weight": latent_output_weight, "anchor": anchor}


EPSILON = 1e-06
NEG_LARGE = -1e+30
GUIDANCE = 3.5
TIME_SHIFT = 3.0

def layer_norm(inputs):
    values = inputs.astype(jnp.float32)
    center = lax.optimization_barrier(jnp.mean(values, axis=-1, keepdims=True))
    spread = lax.optimization_barrier(jnp.mean(jnp.square(values - center), axis=-1, keepdims=True))
    return (values - center) / jnp.sqrt(spread + EPSILON)

def head_norm(inputs, gain_vector, head_size):
    shaped = inputs.astype(jnp.float32).reshape(inputs.shape[:-1] + (-1, head_size))
    rms_value = jnp.sqrt(lax.optimization_barrier(jnp.mean(jnp.square(shaped), axis=-1, keepdims=True)) + EPSILON)
    return (shaped / rms_value * gain_vector).astype(jnp.bfloat16)

def sigma_of(index_values):
    fraction = 1.0 - index_values.astype(jnp.float32) / NSTEPS
    return TIME_SHIFT * fraction / (1.0 + (TIME_SHIFT - 1.0) * fraction)

def reference(hidden, text_states, text_lengths, plan_index, modulation, query_key_value_weight, query_gain, key_gain, attention_output_weight, latent_output_weight, anchor):
    inner = attention_output_weight.shape[0]
    heads = inner // HD
    scale_factor = 1.0 / math.sqrt(HD)
    velocity_list = []
    for window_step in range(WINDOW):
        rows_mod = modulation[window_step]
        normalized_states = (layer_norm(hidden[window_step]) * (1.0 + rows_mod[1]) + rows_mod[0]).astype(jnp.bfloat16)
        branch_list = []
        for branch in range(2):
            projected = jnp.dot(normalized_states[branch], query_key_value_weight, preferred_element_type=jnp.float32).astype(jnp.bfloat16)
            query = head_norm(projected[:, :inner], query_gain, HD)
            image_keys = head_norm(projected[:, inner:2 * inner], key_gain, HD)
            image_values = projected[:, 2 * inner:].reshape(IMG, heads, HD)
            text_keys = head_norm(text_states[window_step, branch, :, :inner], key_gain, HD)
            text_values = text_states[window_step, branch, :, inner:].reshape(TXT, heads, HD)
            all_keys = jnp.concatenate([image_keys, text_keys], axis=0)
            all_values = jnp.concatenate([image_values, text_values], axis=0)
            allowed = jnp.concatenate([jnp.ones((IMG,), dtype=bool), jnp.arange(TXT, dtype=jnp.int32) < text_lengths[branch]])
            scores = jnp.einsum('qhd,khd->hqk', query.astype(jnp.float32), all_keys.astype(jnp.float32)) * scale_factor
            masked = jnp.where(allowed[None, None, :], scores, NEG_LARGE)
            maxima = lax.optimization_barrier(jnp.max(masked, axis=-1, keepdims=True))
            expon = jnp.where(allowed[None, None, :], jnp.exp(masked - maxima), 0.0)
            weights = expon.astype(jnp.bfloat16)
            numerator = jnp.einsum('hqk,khd->qhd', weights.astype(jnp.float32), all_values.astype(jnp.float32))
            denominator = lax.optimization_barrier(jnp.sum(expon, axis=-1)).T
            projected_attention = (numerator / denominator[:, :, None]).astype(jnp.bfloat16).reshape(IMG, inner)
            attention_output = jnp.dot(projected_attention, attention_output_weight, preferred_element_type=jnp.float32)
            second = hidden[window_step, branch].astype(jnp.float32) + rows_mod[2] * attention_output
            final_latent_output = (layer_norm(second) * (1.0 + rows_mod[4]) + rows_mod[3]).astype(jnp.bfloat16)
            branch_list.append(jnp.dot(final_latent_output, latent_output_weight, preferred_element_type=jnp.float32))
        velocity_list.append(branch_list[0] + GUIDANCE * (branch_list[1] - branch_list[0]))
    velocity = jnp.stack(velocity_list, axis=0)
    following = jnp.concatenate([plan_index[1:], jnp.full((1,), NSTEPS, dtype=jnp.int32)]).astype(jnp.int32)
    step_size = sigma_of(following) - sigma_of(plan_index)
    drift = step_size[:, None, None] * velocity
    latents = anchor[None] + jnp.cumsum(drift, axis=0)
    return (velocity, latents)
```

```python
import math

import jax
import jax.numpy as jnp
from jax import lax
from jax.experimental import pallas as pl
from jax.experimental.pallas import tpu as pltpu
from jax.sharding import PartitionSpec as P

NSTEPS = 28
EPSILON = 1e-06
NEG_LARGE = -1e30
GUIDANCE = 3.5
TIME_SHIFT = 3.0
LOG2E = 1.4426950408889634

MESH = pl.DeviceIdType.MESH
BF = jnp.bfloat16
F32 = jnp.float32

D = 2432
NSEQ = 16
NTM = 8
ROWS = 128
TROWS = 16
KEYS = 2048
TKEYS = 256
QB = 512
KC = 256
NT = (((1,), (1,)), ((), ()))

T, KV5, Q5, QP, KVA, KVB, OP, O5 = range(8)


def sigma_of(index_values):
    fraction = 1.0 - index_values / NSTEPS
    return TIME_SHIFT * fraction / (1.0 + (TIME_SHIFT - 1.0) * fraction)


def normalized(x):
    center = jnp.mean(x, axis=-1, keepdims=True)
    x = x - center
    spread = jnp.mean(x * x, axis=-1, keepdims=True)
    return x * lax.rsqrt(spread + EPSILON)


def head_mean_matrix():
    row = lax.broadcasted_iota(jnp.int32, (256, 256), 0) // 64
    col = lax.broadcasted_iota(jnp.int32, (256, 256), 1) // 64
    return jnp.where(row == col, 1.0 / 64, 0.0).astype(BF)


def head_norm(x, gain, mean_matrix):
    square = x * x
    high = square.astype(BF)
    low = (square - high.astype(F32)).astype(BF)
    mean = jnp.dot(high, mean_matrix, preferred_element_type=F32)
    mean += jnp.dot(low, mean_matrix, preferred_element_type=F32)
    return x * lax.rsqrt(mean + EPSILON) * gain


def interleave(keys, values, low_lanes):
    swapped = pltpu.roll(values, 64, 1)
    return jnp.where(low_lanes, keys, swapped), jnp.where(low_lanes, swapped, keys)


def attend(query, image_kv, text_kv, bias, key_lanes):
    query = jnp.where(key_lanes[:1], query, BF(0))
    maxima = total = None
    for start in range(0, KEYS + TKEYS, KC):
        if start < KEYS:
            block = image_kv[start : start + KC, :]
        else:
            block = text_kv[...]
        scores = lax.dot_general(query, block, NT, preferred_element_type=F32)
        if start >= KEYS:
            scores = scores + bias
        largest = jnp.max(scores, axis=1, keepdims=True)
        ones_values = jnp.where(key_lanes, BF(1), block)
        if maxima is None:
            expon = jnp.exp2(scores - largest).astype(BF)
            total = jnp.dot(expon, ones_values, preferred_element_type=F32)
        else:
            largest = jnp.maximum(maxima, largest)
            expon = jnp.exp2(scores - largest).astype(BF)
            total = total * jnp.exp2(maxima - largest) + jnp.dot(
                expon, ones_values, preferred_element_type=F32
            )
        maxima = largest
    return total


def kernel(
    hidden_hbm, text_hbm, lengths, plan, mod_hbm, wqkv_hbm, qgain, kgain, wout_hbm, wlat_hbm, anchor,
    velocity, latents,
    hid, text, mod, wqkv, wout, wlat, normed, h2,
    s_t, s_kv5, s_q5, s_q, s_kva, s_kvb, s_o, s_o5, text_kv,
    r_t, r_kv5, r_q5, r_q, r_kva, r_kvb, r_o5, mixed, res_a,
    drift, r_drift, sig, r_sig, next_sig,
    load_sem, w_sem, send_sem, recv_sem, dsend_sem, drecv_sem, sig_sem,
):
    tm = lax.axis_index("tm")
    me = lax.axis_index("seq")

    def load(source, target, sem):
        return pltpu.make_async_copy(source, target, sem)

    def block_of(slot):
        return 4 if isinstance(slot, int) and slot == 0 else lax.rem(me // 4 + slot - 1, 4)

    def w_load(slot, third):
        column = third * 1280 + block_of(slot) * 256
        if not isinstance(column, int):
            column = pl.multiple_of(column, 256)
        return load(wqkv_hbm.at[:, pl.ds(column, 256)], wqkv.at[slot * 3 + third], w_sem.at[slot * 3 + third])

    hid_load = load(hidden_hbm, hid, load_sem.at[0])
    mod_load = load(mod_hbm, mod, load_sem.at[1])
    text_load = load(text_hbm, text, load_sem.at[2])
    wout_load = load(wout_hbm, wout, load_sem.at[3])
    wlat_load = load(wlat_hbm, wlat, load_sem.at[4])
    hid_load.start()
    mod_load.start()
    for third in range(3):
        w_load(0, third).start()
    text_load.start()
    for slot in range(1, 5):
        for third in range(3):
            w_load(slot, third).start()
    wout_load.start()
    wlat_load.start()

    barrier = pltpu.get_barrier_semaphore()

    def greet_seq(j, carry):
        pl.semaphore_signal(barrier, inc=1, device_id=(tm, lax.rem(me + j, NSEQ)), device_id_type=MESH)
        return carry

    def greet_tm(j, carry):
        pl.semaphore_signal(barrier, inc=1, device_id=(lax.rem(tm + j, NTM), me), device_id_type=MESH)
        return carry

    lax.fori_loop(1, NSEQ, greet_seq, 0)
    lax.fori_loop(1, NTM, greet_tm, 0)

    def source_of(kind, to):
        if kind == T:
            return s_t.at[to]
        if kind == KV5:
            return s_kv5.at[to // 2]
        if kind == Q5:
            return s_q5.at[(to // 4) * 2 + lax.rem(to, 2)]
        if kind == QP:
            return s_q.at[to]
        if kind == KVA:
            return s_kva.at[to]
        if kind == KVB:
            return s_kvb.at[to]
        if kind == OP:
            return s_o.at[pl.ds(pl.multiple_of(to * ROWS, ROWS), ROWS), :]
        return s_o5.at[pl.ds(pl.multiple_of(to * 64, 64), 64), :]

    def target_of(kind, frm):
        rows = pl.ds(pl.multiple_of(frm * ROWS, ROWS), ROWS)
        if kind == T:
            return r_t.at[:, pl.ds(pl.multiple_of(frm * TROWS, TROWS), TROWS), :]
        if kind == KV5:
            return r_kv5.at[rows, :]
        if kind == Q5:
            return r_q5.at[pl.ds(pl.multiple_of(frm * 64, 64), 64), :]
        if kind == QP:
            return r_q.at[rows, :]
        if kind == KVA:
            return r_kva.at[rows, :]
        if kind == KVB:
            return r_kvb.at[rows, :]
        if kind == OP:
            branch = lax.rem(frm // 2, 2)
            pair = 2 * (frm // 4) + lax.rem(frm, 2)
            return mixed.at[pair, pl.ds(pl.multiple_of(branch * ROWS, ROWS), ROWS), :]
        return r_o5.at[frm]

    def transfer(kind, to, frm):
        return pltpu.make_async_remote_copy(
            src_ref=source_of(kind, to),
            dst_ref=target_of(kind, frm),
            send_sem=send_sem.at[kind, to],
            recv_sem=recv_sem.at[kind, frm],
            device_id=(tm, to),
            device_id_type=MESH,
        )

    def send(kind, to):
        @pl.when(to != me)
        def _():
            transfer(kind, to, me).start()

        @pl.when(to == me)
        def _():
            target_of(kind, me)[...] = source_of(kind, me)[...]

    def receive_all(kind):
        def one(j, carry):
            frm = lax.rem(me + j, NSEQ)
            pltpu.make_async_remote_copy(
                src_ref=source_of(kind, frm),
                dst_ref=target_of(kind, frm),
                send_sem=send_sem.at[kind, frm],
                recv_sem=recv_sem.at[kind, frm],
                device_id=(tm, frm),
                device_id_type=MESH,
            ).wait_recv()
            return carry

        lax.fori_loop(1, NSEQ, one, 0)

    low_row = lax.broadcasted_iota(jnp.int32, (1, 128), 1) < 64
    mean_matrix = head_mean_matrix()
    qg = qgain[...] * (LOG2E / math.sqrt(64))
    qg = jnp.concatenate([qg] * 4, axis=1)
    kg = jnp.concatenate([kgain[...]] * 4, axis=1)

    sig[...] = sigma_of(jnp.full((8, 128), plan[0], jnp.int32).astype(F32))
    hid_load.wait()
    mod_load.wait()

    def first_norm(i, carry):
        rows = pl.ds(pl.multiple_of(i * 32, 32), 32)
        x = normalized(hid[rows, :].astype(F32))
        normed[rows, :] = (x * (1.0 + mod[1:2, :]) + mod[0:1, :]).astype(BF)
        return carry

    lax.fori_loop(0, 8, first_norm, 0)

    def project(slot):
        parts = []
        for third in range(3):
            w_load(slot, third).wait()
            part = jnp.dot(normed[...], wqkv[slot * 3 + third], preferred_element_type=F32)
            if third < 2:
                part = part.astype(BF).astype(F32)
                part = head_norm(part, qg if third == 0 else kg, mean_matrix)
            parts.append(part)
        return parts

    q, k, v = project(0)
    for b in range(2):
        for s in range(2):
            lanes = slice(128 * s, 128 * s + 128)
            rows = slice(ROWS * b, ROWS * b + ROWS)
            first, second = interleave(k[rows, lanes], v[rows, lanes], low_row)
            item = (b * 2 + s) * 2
            s_kv5[item] = first.astype(BF)
            s_kv5[item + 1] = second.astype(BF)
            for half in range(2):
                s_q5[item + half] = q[ROWS * b + 64 * half : ROWS * b + 64 * half + 64, lanes].astype(BF)

    pl.semaphore_wait(barrier, NSEQ - 1 + NTM - 1)

    def send_shared(j, carry):
        to = lax.rem(me + j, NSEQ)
        send(KV5, to)
        send(Q5, to)
        return carry

    lax.fori_loop(0, NSEQ, send_shared, 0)

    text_load.wait()
    for c in range(5):
        lanes = slice(256 * c, 256 * c + 256)
        tk = head_norm(text[:, lanes].astype(F32), kg, mean_matrix)
        tv = text[:, 1280 + 256 * c : 1280 + 256 * c + 256].astype(F32)
        for s in range(2):
            sub = slice(128 * s, 128 * s + 128)
            first, second = interleave(tk[:, sub], tv[:, sub], low_row)
            text_kv[4 * c + 2 * s] = first.astype(BF)
            text_kv[4 * c + 2 * s + 1] = second.astype(BF)
    for to in range(NSEQ):
        b, pair = (to // 2) % 2, 2 * (to // 4) + to % 2
        s_t[to, 0] = text_kv[2 * pair, TROWS * b : TROWS * b + TROWS]
        s_t[to, 1] = text_kv[2 * pair + 1, TROWS * b : TROWS * b + TROWS]
        b, head = to // 8, 16 + (to // 2) % 4
        s_t[to, 2] = text_kv[head, TROWS * b : TROWS * b + TROWS]

    def send_text(j, carry):
        send(T, lax.rem(me + j, NSEQ))
        return carry

    lax.fori_loop(0, NSEQ, send_text, 0)

    def sig_copy(to):
        return pltpu.make_async_remote_copy(
            src_ref=sig, dst_ref=r_sig, send_sem=sig_sem.at[0], recv_sem=sig_sem.at[1],
            device_id=(to, me), device_id_type=MESH,
        )

    @pl.when(tm > 0)
    def _():
        sig_copy(tm - 1).start()

    def whole(slot, carry):
        q, k, v = project(slot)
        block = block_of(slot)
        for b in range(2):
            for s in range(2):
                lanes = slice(128 * s, 128 * s + 128)
                rows = slice(ROWS * b, ROWS * b + ROWS)
                to = block * 4 + b * 2 + s
                first, second = interleave(k[rows, lanes], v[rows, lanes], low_row)
                s_q[to] = q[rows, lanes].astype(BF)
                s_kva[to] = first.astype(BF)
                s_kvb[to] = second.astype(BF)
        for part in range(4):
            to = block * 4 + lax.rem(part + me, 4)
            send(QP, to)
            send(KVA, to)
        return carry

    lax.fori_loop(1, 5, whole, 0)

    def send_second(j, carry):
        send(KVB, lax.rem((me // 4) * 4 + j + me, NSEQ))
        return carry

    lax.fori_loop(0, NSEQ, send_second, 0)

    def bias_of(branch):
        key = lax.broadcasted_iota(jnp.int32, (1, TKEYS), 1)
        return jnp.where(key < lengths[branch], 0.0, NEG_LARGE)

    receive_all(KV5)
    receive_all(Q5)
    receive_all(T)
    second_head = lax.rem(me // 2, 2)
    lane = lax.broadcasted_iota(jnp.int32, (KC, 128), 1)
    shared_lanes = (lane // 64) == second_head
    bias5 = bias_of(me // 8)

    def shared_block(i, carry):
        rows = pl.ds(pl.multiple_of(i * QB, QB), QB)
        res = attend(r_q5[rows, :], r_kv5, r_t.at[2], bias5, shared_lanes)
        out = pltpu.roll(res, 64, 1) / res
        s_o5[rows, :] = jnp.where(shared_lanes[:1], out, 0.0).astype(BF)
        for part in range(QB // 64):
            send(O5, i * (QB // 64) + part)
        return carry

    lax.fori_loop(0, 1024 // QB, shared_block, 0)

    receive_all(QP)
    receive_all(KVA)
    bias = bias_of(lax.rem(me // 2, 2))
    low_lanes = lane < 64

    def first_block(i, carry):
        rows = pl.ds(pl.multiple_of(i * QB, QB), QB)
        res_a[rows, :] = attend(r_q[rows, :], r_kva, r_t.at[0], bias, low_lanes)
        return carry

    lax.fori_loop(0, KEYS // QB, first_block, 0)

    receive_all(KVB)
    high_lanes = lane >= 64

    def second_block(j, carry):
        i = lax.rem(j + me // 4, KEYS // QB)
        rows = pl.ds(pl.multiple_of(i * QB, QB), QB)
        second = attend(r_q[rows, :], r_kvb, r_t.at[1], bias, high_lanes)
        first = res_a[rows, :]
        above = jnp.where(low_row, second, first)
        below = jnp.where(low_row, first, second)
        s_o[rows, :] = (pltpu.roll(above, 64, 1) / below).astype(BF)
        for part in range(QB // ROWS):
            send(OP, i * (QB // ROWS) + part)
        return carry

    lax.fori_loop(0, KEYS // QB, second_block, 0)

    receive_all(O5)
    for b in range(2):
        for s in range(2):
            for half in range(2):
                first = (b * 2 + s) * 4 + half
                mixed[8 + s, ROWS * b + 64 * half : ROWS * b + 64 * half + 64, :] = r_o5[first] + r_o5[first + 2]
    wout_load.wait()
    wlat_load.wait()
    receive_all(OP)

    gathered = jnp.concatenate([mixed[i] for i in range(10)], axis=1)
    for start in range(0, D, 512):
        stop = min(D, start + 512)
        out = jnp.dot(gathered, wout[:, start:stop], preferred_element_type=F32)
        h2[:, start:stop] = hid[:, start:stop].astype(F32) + mod[2:3, start:stop] * out

    def second_norm(i, carry):
        rows = pl.ds(pl.multiple_of(i * 32, 32), 32)
        x = normalized(h2[rows, :])
        normed[rows, :] = (x * (1.0 + mod[4:5, :]) + mod[3:4, :]).astype(BF)
        return carry

    lax.fori_loop(0, 8, second_norm, 0)
    branches = jnp.dot(normed[...], wlat[...], preferred_element_type=F32)
    guided = branches[:ROWS] + GUIDANCE * (branches[ROWS:] - branches[:ROWS])
    velocity[...] = guided

    @pl.when(tm < NTM - 1)
    def _():
        sig_copy(tm).wait_recv()
        next_sig[...] = r_sig[...]

    @pl.when(tm == NTM - 1)
    def _():
        next_sig[...] = jnp.zeros_like(next_sig)

    step = (next_sig[...] - sig[...])[0:1, 0:64]
    drift[...] = step * guided

    def drift_copy(to, frm):
        return pltpu.make_async_remote_copy(
            src_ref=drift, dst_ref=r_drift.at[frm], send_sem=dsend_sem.at[to], recv_sem=drecv_sem.at[frm],
            device_id=(to, me), device_id_type=MESH,
        )

    for to in range(1, NTM):
        @pl.when(to > tm)
        def _():
            drift_copy(to, tm).start()

    latents[...] = anchor[...] + drift[...]
    for frm in range(NTM - 1):
        @pl.when(frm < tm)
        def _():
            drift_copy(frm, frm).wait_recv()
            latents[...] += r_drift[frm]

    for to in range(1, NTM):
        @pl.when(to > tm)
        def _():
            drift_copy(to, tm).wait_send()

    @pl.when(tm > 0)
    def _():
        sig_copy(tm - 1).wait_send()

    for kind in range(8):
        def done(j, carry):
            transfer(kind, lax.rem(me + j, NSEQ), me).wait_send()
            return carry

        lax.fori_loop(1, NSEQ, done, 0)


def on_device(
    hidden, text_states, text_lengths, plan_index, modulation, query_key_value_weight, query_gain, key_gain,
    attention_output_weight, latent_output_weight, anchor,
):
    any_spec = pl.BlockSpec(memory_space=pl.ANY)
    vmem = pl.BlockSpec(memory_space=pltpu.VMEM)
    smem = pl.BlockSpec(memory_space=pltpu.SMEM)
    tile = lambda *lead: pltpu.VMEM(lead + (128, 128), BF)
    velocity, latents = pl.pallas_call(
        kernel,
        out_shape=[jax.ShapeDtypeStruct((ROWS, 64), F32)] * 2,
        in_specs=[any_spec, any_spec, smem, smem, any_spec, any_spec, vmem, vmem, any_spec, any_spec, vmem],
        out_specs=[vmem, vmem],
        scratch_shapes=[
            pltpu.VMEM((256, D), BF),
            pltpu.VMEM((32, 2560), BF),
            pltpu.VMEM((5, D), F32),
            pltpu.VMEM((15, D, 256), BF),
            pltpu.VMEM((1280, D), BF),
            pltpu.VMEM((D, 64), BF),
            pltpu.VMEM((256, D), BF),
            pltpu.VMEM((256, D), F32),
            pltpu.VMEM((16, 3, TROWS, 128), BF),
            tile(8),
            pltpu.VMEM((8, 64, 128), BF),
            tile(16),
            tile(16),
            tile(16),
            pltpu.VMEM((KEYS, 128), BF),
            pltpu.VMEM((1024, 128), BF),
            pltpu.VMEM((20, 32, 128), BF),
            pltpu.VMEM((3, TKEYS, 128), BF),
            pltpu.VMEM((KEYS, 128), BF),
            pltpu.VMEM((1024, 128), BF),
            pltpu.VMEM((KEYS, 128), BF),
            pltpu.VMEM((KEYS, 128), BF),
            pltpu.VMEM((KEYS, 128), BF),
            pltpu.VMEM((16, 64, 128), BF),
            pltpu.VMEM((10, 256, 128), BF),
            pltpu.VMEM((KEYS, 128), F32),
            pltpu.VMEM((ROWS, 64), F32),
            pltpu.VMEM((NTM, ROWS, 64), F32),
            pltpu.VMEM((8, 128), F32),
            pltpu.VMEM((8, 128), F32),
            pltpu.VMEM((8, 128), F32),
            pltpu.SemaphoreType.DMA((5,)),
            pltpu.SemaphoreType.DMA((15,)),
            pltpu.SemaphoreType.DMA((8, NSEQ)),
            pltpu.SemaphoreType.DMA((8, NSEQ)),
            pltpu.SemaphoreType.DMA((NTM,)),
            pltpu.SemaphoreType.DMA((NTM,)),
            pltpu.SemaphoreType.DMA((2,)),
        ],
        compiler_params=pltpu.CompilerParams(
            collective_id=0, has_side_effects=True, vmem_limit_bytes=58 * 2**20
        ),
        cost_estimate=pl.CostEstimate(flops=9_600_000_000, bytes_accessed=28_000_000, transcendentals=12_000_000),
    )(
        hidden.reshape(256, D),
        text_states.reshape(32, 2560),
        text_lengths,
        plan_index,
        modulation[0],
        query_key_value_weight,
        query_gain[None],
        key_gain[None],
        attention_output_weight,
        latent_output_weight,
        anchor,
    )
    return velocity[None], latents[None]


def solution(mesh):
    in_specs = (
        P("tm", None, "seq", None),
        P("tm", None, "seq", None),
        P(),
        P("tm"),
        P("tm", None, None),
        P(),
        P(),
        P(),
        P(),
        P(),
        P("seq", None),
    )
    out_specs = (P("tm", "seq", None), P("tm", "seq", None))
    return jax.shard_map(
        on_device, mesh=mesh, in_specs=in_specs, out_specs=out_specs, check_vma=False
    )
```

```python
import math

import jax
import jax.numpy as jnp
from jax import lax
from jax.experimental import pallas as pl
from jax.experimental.pallas import tpu as pltpu
from jax.sharding import PartitionSpec as P

NSTEPS = 28
EPSILON = 1e-06
NEG_LARGE = -1e30
GUIDANCE = 3.5
TIME_SHIFT = 3.0
LOG2E = 1.4426950408889634

MESH = pl.DeviceIdType.MESH
BF = jnp.bfloat16
F32 = jnp.float32

D = 2432
NSEQ = 16
NTM = 8
ROWS = 128
TROWS = 16
KEYS = 2048
TKEYS = 256
QB = 512
KC = 256
NT = (((1,), (1,)), ((), ()))

OTHERS = sorted(
    ((dz, dy) for dz in range(4) for dy in range(4) if dz or dy),
    key=lambda step: -(min(step[0], 4 - step[0]) + min(step[1], 4 - step[1])),
)

T, KV5, Q5, QP, KVA, KVB, OP, O5 = range(8)


def sigma_of(index_values):
    fraction = 1.0 - index_values / NSTEPS
    return TIME_SHIFT * fraction / (1.0 + (TIME_SHIFT - 1.0) * fraction)


def normalized(x):
    center = jnp.mean(x, axis=-1, keepdims=True)
    x = x - center
    spread = jnp.mean(x * x, axis=-1, keepdims=True)
    return x * lax.rsqrt(spread + EPSILON)


def head_mean_matrix():
    row = lax.broadcasted_iota(jnp.int32, (256, 256), 0) >> 6
    col = lax.broadcasted_iota(jnp.int32, (256, 256), 1) >> 6
    return jnp.where(row == col, 1.0 / 64, 0.0).astype(BF)


def head_norm(x, gain, mean_matrix):
    square = x * x
    high = square.astype(BF)
    low = (square - high.astype(F32)).astype(BF)
    mean = jnp.dot(high, mean_matrix, preferred_element_type=F32)
    mean += jnp.dot(low, mean_matrix, preferred_element_type=F32)
    return x * lax.rsqrt(mean + EPSILON) * gain


def swap(x):
    return pltpu.roll(x, 64, 1)


def interleave(keys, values, low_lanes):
    swapped = swap(values)
    return jnp.where(low_lanes, keys, swapped), jnp.where(low_lanes, swapped, keys)


def keys_first(keys, values, low_lanes):
    return jnp.where(low_lanes, keys, swap(values)), jnp.where(low_lanes, swap(keys), values)


def attend(query, image_kv, text_kv, bias, key_lanes):
    query = jnp.where(key_lanes[:1], query, BF(0))
    maxima = total = None
    for start in range(0, KEYS + TKEYS, KC):
        if start < KEYS:
            block = image_kv[start : start + KC, :]
        else:
            block = text_kv[...]
        scores = lax.dot_general(query, block, NT, preferred_element_type=F32)
        if start >= KEYS:
            scores = scores + bias
        largest = jnp.max(scores, axis=1, keepdims=True)
        ones_values = jnp.where(key_lanes, BF(1), block)
        if maxima is None:
            expon = jnp.exp2(scores - largest).astype(BF)
            total = jnp.dot(expon, ones_values, preferred_element_type=F32)
        else:
            largest = jnp.maximum(maxima, largest)
            expon = jnp.exp2(scores - largest).astype(BF)
            total = total * jnp.exp2(maxima - largest) + jnp.dot(
                expon, ones_values, preferred_element_type=F32
            )
        maxima = largest
    return total


def guide(branches):
    return branches[:, :ROWS] + GUIDANCE * (branches[:, ROWS:] - branches[:, :ROWS])


def finish(branches, total, anchor, velocity, latents):
    velocity[...] = guide(branches[...])
    latents[...] = anchor[...] + total[...]


def kernel(
    hidden_hbm, text_hbm, lengths, plan, mod_hbm, wqkv_hbm, qgain, kgain, wout_hbm, wlat_hbm,
    branches_out, total,
    hid, text, mod, wqkv, wout, wlat, normed, h2,
    s_t, s_kv5, s_q5, s_q, s_kva, s_kvb, s_o, s_o5, text_kv,
    r_t, r_kv5, r_q5, r_q, r_kva, r_kvb, r_o5, mixed, res_a,
    drift, r_drift, sig, r_sig, next_sig,
    load_sem, w_sem, send_sem, recv_sem, dsend_sem, drecv_sem, sig_sem,
):
    tm = lax.axis_index("tm")
    me = lax.axis_index("seq")
    my_z, my_y = me // 4, lax.rem(me, 4)

    def owner(block, z):
        return z * 4 + lax.rem(block + 4 - z, 4)

    def pair_of(device):
        z = device // 4
        block = lax.rem(z + lax.rem(device, 4), 4)
        return z // 2, 2 * block + lax.rem(z, 2)

    odd = lax.rem(my_z + my_y + tm, 2)

    def extra_owners():
        for dz in (2, 1, 3, 0):
            for far in (1, 0):
                dy = 2 * far + lax.rem(dz + odd, 2)
                yield lax.rem(my_z + dz, 4) * 4 + lax.rem(my_y + dy, 4)

    def extra_item(device):
        return (device // 4) * 2 + lax.rem(device, 4) // 2

    def extra_owner(item):
        z = item // 2
        return z * 4 + 2 * (item % 2) + lax.rem(z + tm, 2)

    def others():
        for dz, dy in OTHERS:
            yield lax.rem(my_z + dz, 4) * 4 + lax.rem(my_y + dy, 4)

    def load(source, target, sem):
        return pltpu.make_async_copy(source, target, sem)

    def block_of(slot):
        if isinstance(slot, int) and slot == 0:
            return 4
        return jnp.where(slot == 0, 4, lax.rem(my_z + my_y + slot + 1, 4))

    def w_load(slot, third):
        column = third * 1280 + block_of(slot) * 256
        if not isinstance(column, int):
            column = pl.multiple_of(column, 256)
        return load(wqkv_hbm.at[:, pl.ds(column, 256)], wqkv.at[slot * 3 + third], w_sem.at[slot * 3 + third])

    hid_load = load(hidden_hbm, hid, load_sem.at[0])
    mod_load = load(mod_hbm, mod, load_sem.at[1])
    text_load = load(text_hbm, text, load_sem.at[2])
    wout_load = load(wout_hbm, wout, load_sem.at[3])
    wlat_load = load(wlat_hbm, wlat, load_sem.at[4])
    hid_load.start()
    mod_load.start()
    for third in range(3):
        w_load(0, third).start()
    text_load.start()

    barrier = pltpu.get_barrier_semaphore()

    def greet_seq(j, carry):
        pl.semaphore_signal(barrier, inc=1, device_id=(tm, lax.rem(me + j, NSEQ)), device_id_type=MESH)
        return carry

    def greet_tm(j, carry):
        pl.semaphore_signal(barrier, inc=1, device_id=(lax.rem(tm + j, NTM), me), device_id_type=MESH)
        return carry

    lax.fori_loop(1, NSEQ, greet_seq, 0)
    lax.fori_loop(1, NTM, greet_tm, 0)

    def query_rows(device):
        z = device // 4
        place = lax.rem(z + lax.rem(device, 4), 4) * 4 + z
        return pl.ds(pl.multiple_of(place * ROWS, ROWS), ROWS)

    def source_of(kind, to):
        if kind == T:
            return s_t.at[to]
        if kind == KV5:
            return s_kv5.at[extra_item(to)]
        if kind == Q5:
            return s_q5.at[extra_item(to)]
        if kind == QP:
            return s_q.at[to]
        if kind == KVA:
            return s_kva.at[to]
        if kind == KVB:
            return s_kvb.at[to]
        if kind == OP:
            return s_o.at[query_rows(to), :]
        return s_o5.at[pl.ds(pl.multiple_of(to * 64, 64), 64), :]

    def target_of(kind, frm):
        rows = pl.ds(pl.multiple_of(frm * ROWS, ROWS), ROWS)
        if kind == T:
            return r_t.at[:, pl.ds(pl.multiple_of(frm * TROWS, TROWS), TROWS), :]
        if kind == KV5:
            return r_kv5.at[rows, :]
        if kind == Q5:
            return r_q5.at[pl.ds(pl.multiple_of(frm * 64, 64), 64), :]
        if kind == QP:
            return r_q.at[query_rows(frm), :]
        if kind == KVA:
            return r_kva.at[rows, :]
        if kind == KVB:
            return r_kvb.at[rows, :]
        if kind == OP:
            branch, pair = pair_of(frm)
            return mixed.at[pair, pl.ds(pl.multiple_of(branch * ROWS, ROWS), ROWS), :]
        return r_o5.at[extra_item(frm)]

    def transfer(kind, to, frm):
        return pltpu.make_async_remote_copy(
            src_ref=source_of(kind, to),
            dst_ref=target_of(kind, frm),
            send_sem=send_sem.at[kind, to],
            recv_sem=recv_sem.at[kind, frm],
            device_id=(tm, to),
            device_id_type=MESH,
        )

    def keep(kind):
        target_of(kind, me)[...] = source_of(kind, me)[...]

    def send(kind, to):
        @pl.when(to != me)
        def _():
            transfer(kind, to, me).start()

        @pl.when(to == me)
        def _():
            keep(kind)

    def receive_all(kind):
        def one(j, carry):
            frm = lax.rem(me + j, NSEQ)
            pltpu.make_async_remote_copy(
                src_ref=source_of(kind, frm),
                dst_ref=target_of(kind, frm),
                send_sem=send_sem.at[kind, frm],
                recv_sem=recv_sem.at[kind, frm],
                device_id=(tm, frm),
                device_id_type=MESH,
            ).wait_recv()
            return carry

        lax.fori_loop(1, NSEQ, one, 0)

    low_row = lax.broadcasted_iota(jnp.int32, (1, 128), 1) < 64
    mean_matrix = head_mean_matrix()
    qg = qgain[...] * (LOG2E / math.sqrt(64))
    qg = jnp.concatenate([qg] * 4, axis=1)
    kg = jnp.concatenate([kgain[...]] * 4, axis=1)

    sig[...] = sigma_of(jnp.full((8, 128), plan[0], jnp.int32).astype(F32))
    hid_load.wait()
    mod_load.wait()

    def first_norm(i, carry):
        rows = pl.ds(pl.multiple_of(i * 32, 32), 32)
        x = normalized(hid[rows, :].astype(F32))
        normed[rows, :] = (x * (1.0 + mod[1]) + mod[0]).astype(BF)
        return carry

    lax.fori_loop(0, 8, first_norm, 0)

    def project(slot):
        parts = []
        for third in range(3):
            w_load(slot, third).wait()

            @pl.when(slot < 4)
            def _():
                w_load(slot + 1, third).start()

            part = jnp.dot(normed[...], wqkv[slot * 3 + third], preferred_element_type=F32)
            if third < 2:
                part = part.astype(BF).astype(F32)
                part = head_norm(part, qg if third == 0 else kg, mean_matrix)
            parts.append(part)
        return parts

    q, k, v = project(jnp.int32(0))
    for b in range(2):
        for s in range(2):
            lanes = slice(128 * s, 128 * s + 128)
            rows = slice(ROWS * b, ROWS * b + ROWS)
            first, second = keys_first(k[rows, lanes], v[rows, lanes], low_row)
            item = (b * 2 + s) * 2
            s_kv5[item] = first.astype(BF)
            s_kv5[item + 1] = second.astype(BF)
            above = q[ROWS * b : ROWS * b + 64, lanes]
            below = q[ROWS * b + 64 : ROWS * b + ROWS, lanes]
            s_q5[item] = jnp.where(low_row, above, swap(below)).astype(BF)
            s_q5[item + 1] = jnp.where(low_row, swap(above), below).astype(BF)

    pl.semaphore_wait(barrier, NSEQ - 1 + NTM - 1)

    for to in extra_owners():
        send(KV5, to)
        send(Q5, to)

    text_load.wait()
    for c in range(5):
        lanes = slice(256 * c, 256 * c + 256)
        tk = head_norm(text[:, lanes].astype(F32), kg, mean_matrix)
        tv = text[:, 1280 + 256 * c : 1280 + 256 * c + 256].astype(F32)
        for s in range(2):
            sub = slice(128 * s, 128 * s + 128)
            arrange = keys_first if c == 4 else interleave
            first, second = arrange(tk[:, sub], tv[:, sub], low_row)
            text_kv[4 * c + 2 * s] = first.astype(BF)
            text_kv[4 * c + 2 * s + 1] = second.astype(BF)
    for to in range(NSEQ):
        b, pair = to // 8, 2 * ((to // 4 + to) % 4) + (to // 4) % 2
        s_t[to, 0] = text_kv[2 * pair, TROWS * b : TROWS * b + TROWS]
        s_t[to, 1] = text_kv[2 * pair + 1, TROWS * b : TROWS * b + TROWS]
        item = (to // 4) * 2 + (to % 4) // 2
        b, head = item // 4, 16 + item % 4
        s_t[to, 2] = text_kv[head, TROWS * b : TROWS * b + TROWS]

    for to in others():
        transfer(T, to, me).start()
    keep(T)

    def sig_copy(to):
        return pltpu.make_async_remote_copy(
            src_ref=sig, dst_ref=r_sig, send_sem=sig_sem.at[0], recv_sem=sig_sem.at[1],
            device_id=(to, me), device_id_type=MESH,
        )

    @pl.when(tm > 0)
    def _():
        sig_copy(tm - 1).start()

    def whole(slot, carry):
        q, k, v = project(slot)
        block = block_of(slot)
        for b in range(2):
            for s in range(2):
                lanes = slice(128 * s, 128 * s + 128)
                rows = slice(ROWS * b, ROWS * b + ROWS)
                to = owner(block, 2 * b + s)
                first, second = interleave(k[rows, lanes], v[rows, lanes], low_row)
                s_q[to] = q[rows, lanes].astype(BF)
                s_kva[to] = first.astype(BF)
                s_kvb[to] = second.astype(BF)
        for dz in (2, 1, 3, 0):
            to = owner(block, lax.rem(my_z + dz, 4))
            send(QP, to)
            send(KVA, to)
        return carry

    lax.fori_loop(1, 5, whole, 0)
    wout_load.start()
    wlat_load.start()

    for to in others():
        transfer(KVB, to, me).start()
    keep(KVB)

    def bias_of(branch):
        key = lax.broadcasted_iota(jnp.int32, (1, TKEYS), 1)
        return jnp.where(key < lengths[branch], 0.0, NEG_LARGE)

    lane = lax.broadcasted_iota(jnp.int32, (KC, 128), 1)
    low_lanes, high_lanes = lane < 64, lane >= 64
    bias = bias_of(me // 8)
    receive_all(T)

    @pl.when(odd == 0)
    def _():
        receive_all(KV5)
        receive_all(Q5)

        def extra_block(i, carry):
            rows = pl.ds(pl.multiple_of(i * QB, QB), QB)
            packed = r_q5[rows, :]
            first = attend(packed, r_kv5, r_t.at[2], bias, low_lanes)
            second = attend(swap(packed.astype(F32)).astype(BF), r_kv5, r_t.at[2], bias, low_lanes)
            above = jnp.where(low_row, swap(first), second)
            below = jnp.where(low_row, first, swap(second))
            s_o5[rows, :] = (above / below).astype(BF)
            return carry

        lax.fori_loop(0, 1024 // QB, extra_block, 0)
        for to in others():
            transfer(O5, to, me).start()
        keep(O5)

    receive_all(QP)
    receive_all(KVA)

    def first_block(i, carry):
        rows = pl.ds(pl.multiple_of(i * QB, QB), QB)
        res_a[rows, :] = attend(r_q[rows, :], r_kva, r_t.at[0], bias, low_lanes)
        return carry

    lax.fori_loop(0, KEYS // QB, first_block, 0)

    receive_all(KVB)

    def second_block(j, carry):
        i = lax.rem(j + my_z + my_y + 2, 4)
        rows = pl.ds(pl.multiple_of(i * QB, QB), QB)
        second = attend(r_q[rows, :], r_kvb, r_t.at[1], bias, high_lanes)
        first = res_a[rows, :]
        above = jnp.where(low_row, second, first)
        below = jnp.where(low_row, first, second)
        s_o[rows, :] = (swap(above) / below).astype(BF)
        for dz in (2, 1, 3, 0):
            send(OP, owner(i, lax.rem(my_z + dz, 4)))
        return carry

    lax.fori_loop(0, KEYS // QB, second_block, 0)

    for item in range(8):
        frm = extra_owner(item)

        @pl.when(frm != me)
        def _():
            transfer(O5, frm, frm).wait_recv()

    for b in range(2):
        for s in range(2):
            item = (b * 2 + s) * 2
            first = r_o5[item].astype(F32)
            second = r_o5[item + 1].astype(F32)
            start = ROWS * b
            mixed[8 + s, start : start + 64, :] = jnp.where(low_row, first, swap(second)).astype(BF)
            mixed[8 + s, start + 64 : start + ROWS, :] = jnp.where(low_row, swap(first), second).astype(BF)
    wout_load.wait()
    wlat_load.wait()
    receive_all(OP)

    gathered = jnp.concatenate([mixed[i] for i in range(10)], axis=1)
    for start in range(0, D, 512):
        stop = min(D, start + 512)
        out = jnp.dot(gathered, wout[:, start:stop], preferred_element_type=F32)
        h2[:, start:stop] = hid[:, start:stop].astype(F32) + mod[2, :, start:stop] * out

    def second_norm(i, carry):
        rows = pl.ds(pl.multiple_of(i * 32, 32), 32)
        x = normalized(h2[rows, :])
        normed[rows, :] = (x * (1.0 + mod[4]) + mod[3]).astype(BF)
        return carry

    lax.fori_loop(0, 8, second_norm, 0)
    branches = lax.dot_general(wlat[...], normed[...], NT, preferred_element_type=F32)
    guided = guide(branches)
    branches_out[...] = branches

    @pl.when(tm < NTM - 1)
    def _():
        sig_copy(tm).wait_recv()
        next_sig[...] = r_sig[...]

    @pl.when(tm == NTM - 1)
    def _():
        next_sig[...] = jnp.zeros_like(next_sig)

    step = (next_sig[...] - sig[...])[0:1, :]
    drift[...] = step * guided

    def drift_copy(to, frm):
        return pltpu.make_async_remote_copy(
            src_ref=drift, dst_ref=r_drift.at[frm], send_sem=dsend_sem.at[to], recv_sem=drecv_sem.at[frm],
            device_id=(to, me), device_id_type=MESH,
        )

    for to in range(1, NTM):
        @pl.when(to > tm)
        def _():
            drift_copy(to, tm).start()

    total[...] = drift[...]
    for frm in range(NTM - 1):
        @pl.when(frm < tm)
        def _():
            drift_copy(frm, frm).wait_recv()
            total[...] += r_drift[frm]

    for to in range(1, NTM):
        @pl.when(to > tm)
        def _():
            drift_copy(to, tm).wait_send()

    @pl.when(tm > 0)
    def _():
        sig_copy(tm - 1).wait_send()

    for kind in (T, QP, KVA, KVB, OP):
        def done(j, carry):
            transfer(kind, lax.rem(me + j, NSEQ), me).wait_send()
            return carry

        lax.fori_loop(1, NSEQ, done, 0)
    for kind in (KV5, Q5):
        for item in range(8):
            to = extra_owner(item)

            @pl.when(to != me)
            def _():
                transfer(kind, to, me).wait_send()

    @pl.when(odd == 0)
    def _():
        def done(j, carry):
            transfer(O5, lax.rem(me + j, NSEQ), me).wait_send()
            return carry

        lax.fori_loop(1, NSEQ, done, 0)


def on_device(
    hidden, text_states, text_lengths, plan_index, modulation, query_key_value_weight, query_gain, key_gain,
    attention_output_weight, latent_output_weight, anchor,
):
    any_spec = pl.BlockSpec(memory_space=pl.ANY)
    vmem = pl.BlockSpec(memory_space=pltpu.VMEM)
    smem = pl.BlockSpec(memory_space=pltpu.SMEM)
    tile = lambda *lead: pltpu.VMEM(lead + (128, 128), BF)
    branches, total = pl.pallas_call(
        kernel,
        out_shape=[jax.ShapeDtypeStruct((64, 2 * ROWS), F32), jax.ShapeDtypeStruct((64, ROWS), F32)],
        in_specs=[any_spec, any_spec, smem, smem, any_spec, any_spec, vmem, vmem, any_spec, any_spec],
        out_specs=[vmem, vmem],
        scratch_shapes=[
            pltpu.VMEM((256, D), BF),
            pltpu.VMEM((32, 2560), BF),
            pltpu.VMEM((5, 1, D), F32),
            pltpu.VMEM((15, D, 256), BF),
            pltpu.VMEM((1280, D), BF),
            pltpu.VMEM((64, D), BF),
            pltpu.VMEM((256, D), BF),
            pltpu.VMEM((256, D), F32),
            pltpu.VMEM((16, 3, TROWS, 128), BF),
            tile(8),
            pltpu.VMEM((8, 64, 128), BF),
            tile(16),
            tile(16),
            tile(16),
            pltpu.VMEM((KEYS, 128), BF),
            pltpu.VMEM((1024, 128), BF),
            pltpu.VMEM((20, 32, 128), BF),
            pltpu.VMEM((3, TKEYS, 128), BF),
            pltpu.VMEM((KEYS, 128), BF),
            pltpu.VMEM((1024, 128), BF),
            pltpu.VMEM((KEYS, 128), BF),
            pltpu.VMEM((KEYS, 128), BF),
            pltpu.VMEM((KEYS, 128), BF),
            pltpu.VMEM((8, 64, 128), BF),
            pltpu.VMEM((10, 256, 128), BF),
            pltpu.VMEM((KEYS, 128), F32),
            pltpu.VMEM((64, ROWS), F32),
            pltpu.VMEM((NTM, 64, ROWS), F32),
            pltpu.VMEM((8, 128), F32),
            pltpu.VMEM((8, 128), F32),
            pltpu.VMEM((8, 128), F32),
            pltpu.SemaphoreType.DMA((5,)),
            pltpu.SemaphoreType.DMA((15,)),
            pltpu.SemaphoreType.DMA((8, NSEQ)),
            pltpu.SemaphoreType.DMA((8, NSEQ)),
            pltpu.SemaphoreType.DMA((NTM,)),
            pltpu.SemaphoreType.DMA((NTM,)),
            pltpu.SemaphoreType.DMA((2,)),
        ],
        compiler_params=pltpu.CompilerParams(
            collective_id=0, has_side_effects=True, vmem_limit_bytes=58 * 2**20
        ),
        cost_estimate=pl.CostEstimate(flops=9_600_000_000, bytes_accessed=28_000_000, transcendentals=12_000_000),
    )(
        hidden.reshape(256, D),
        text_states.reshape(32, 2560),
        text_lengths,
        plan_index,
        modulation.transpose(1, 0, 2),
        query_key_value_weight,
        query_gain[None],
        key_gain[None],
        attention_output_weight,
        latent_output_weight.T,
    )
    velocity, latents = pl.pallas_call(
        finish,
        out_shape=[jax.ShapeDtypeStruct((64, ROWS), F32)] * 2,
        in_specs=[vmem] * 3,
        out_specs=[vmem] * 2,
    )(branches, total, anchor.T)
    return velocity.T[None], latents.T[None]


def solution(mesh):
    in_specs = (
        P("tm", None, "seq", None),
        P("tm", None, "seq", None),
        P(),
        P("tm"),
        P("tm", None, None),
        P(),
        P(),
        P(),
        P(),
        P(),
        P("seq", None),
    )
    out_specs = (P("tm", "seq", None), P("tm", "seq", None))
    return jax.shard_map(
        on_device, mesh=mesh, in_specs=in_specs, out_specs=out_specs, check_vma=False
    )
```

```python
import math

import jax
import jax.numpy as jnp
from jax import lax
from jax.experimental import pallas as pl
from jax.experimental.pallas import tpu as pltpu
from jax.sharding import PartitionSpec as P

NSTEPS = 28
EPSILON = 1e-06
NEG_LARGE = -1e30
GUIDANCE = 3.5
TIME_SHIFT = 3.0
LOG2E = 1.4426950408889634

MESH = pl.DeviceIdType.MESH
BF = jnp.bfloat16
F32 = jnp.float32

D = 2432
NSEQ = 16
NTM = 8
ROWS = 128
TROWS = 16
KEYS = 2048
TKEYS = 256
QB = 1024
KC = 256
NT = (((1,), (1,)), ((), ()))

OTHERS = sorted(
    ((dz, dy) for dz in range(4) for dy in range(4) if dz or dy),
    key=lambda step: -(min(step[0], 4 - step[0]) + min(step[1], 4 - step[1])),
)

T, KV5, Q5, QP, KVA, KVB, OP, O5 = range(8)


def sigma_of(index_values):
    fraction = 1.0 - index_values / NSTEPS
    return TIME_SHIFT * fraction / (1.0 + (TIME_SHIFT - 1.0) * fraction)


def normalized(x):
    center = jnp.mean(x, axis=-1, keepdims=True)
    x = x - center
    spread = jnp.mean(x * x, axis=-1, keepdims=True)
    return x * lax.rsqrt(spread + EPSILON)


def head_mean_matrix():
    row = lax.broadcasted_iota(jnp.int32, (256, 256), 0) >> 6
    col = lax.broadcasted_iota(jnp.int32, (256, 256), 1) >> 6
    return jnp.where(row == col, 1.0 / 64, 0.0).astype(BF)


def head_norm(x, gain, mean_matrix):
    square = x * x
    high = square.astype(BF)
    low = (square - high.astype(F32)).astype(BF)
    mean = jnp.dot(high, mean_matrix, preferred_element_type=F32)
    mean += jnp.dot(low, mean_matrix, preferred_element_type=F32)
    return x * lax.rsqrt(mean + EPSILON) * gain


def swap(x):
    return pltpu.roll(x, 64, 1)


def interleave(keys, values, low_lanes):
    swapped = swap(values)
    return jnp.where(low_lanes, keys, swapped), jnp.where(low_lanes, swapped, keys)


def keys_first(keys, values, low_lanes):
    return jnp.where(low_lanes, keys, swap(values)), jnp.where(low_lanes, swap(keys), values)


def attend(query, image_kv, text_kv, bias, key_lanes):
    query = jnp.where(key_lanes[:1], query, BF(0))
    maxima = total = None
    for start in range(0, KEYS + TKEYS, KC):
        if start < KEYS:
            block = image_kv[start : start + KC, :]
        else:
            block = text_kv[...]
        scores = lax.dot_general(query, block, NT, preferred_element_type=F32)
        if start >= KEYS:
            scores = scores + bias
        largest = jnp.max(scores, axis=1, keepdims=True)
        ones_values = jnp.where(key_lanes, BF(1), block)
        if maxima is None:
            expon = jnp.exp2(scores - largest).astype(BF)
            total = jnp.dot(expon, ones_values, preferred_element_type=F32)
        else:
            largest = jnp.maximum(maxima, largest)
            expon = jnp.exp2(scores - largest).astype(BF)
            total = total * jnp.exp2(maxima - largest) + jnp.dot(
                expon, ones_values, preferred_element_type=F32
            )
        maxima = largest
    return total


def guide(branches):
    return branches[:, :ROWS] + GUIDANCE * (branches[:, ROWS:] - branches[:, :ROWS])


def finish(branches, total, anchor, velocity, latents):
    velocity[...] = guide(branches[...])
    latents[...] = anchor[...] + total[...]


def kernel(
    hidden_hbm, text_hbm, lengths, plan, mod_hbm, wqkv_hbm, qgain, kgain, wout_hbm, wlat_hbm,
    branches_out, total,
    hid, text, mod, wqkv, wout, wlat, normed, h2,
    s_t, s_kv5, s_q5, s_q, s_kva, s_kvb, s_o, s_o5, text_kv,
    r_t, r_kv5, r_qx, r_q5, r_q, r_kva, r_kvb, r_o5, mixed, res_a,
    drift, r_drift, sig, r_sig, next_sig,
    load_sem, w_sem, send_sem, recv_sem, dsend_sem, drecv_sem, sig_sem,
):
    tm = lax.axis_index("tm")
    me = lax.axis_index("seq")
    my_z, my_y = me // 4, lax.rem(me, 4)

    def owner(block, z):
        return z * 4 + lax.rem(block + 4 - z, 4)

    def pair_of(device):
        z = device // 4
        block = lax.rem(z + lax.rem(device, 4), 4)
        return z // 2, 2 * block + lax.rem(z, 2)

    odd = lax.rem(my_z + my_y + tm, 2)

    def extra_owners():
        for dz in (2, 1, 3, 0):
            for far in (1, 0):
                dy = 2 * far + lax.rem(dz + odd, 2)
                yield lax.rem(my_z + dz, 4) * 4 + lax.rem(my_y + dy, 4)

    def extra_item(device):
        return (device // 4) * 2 + lax.rem(device, 4) // 2

    def extra_owner(item):
        z = item // 2
        return z * 4 + 2 * (item % 2) + lax.rem(z + tm, 2)

    def others():
        for dz, dy in OTHERS:
            yield lax.rem(my_z + dz, 4) * 4 + lax.rem(my_y + dy, 4)

    def load(source, target, sem):
        return pltpu.make_async_copy(source, target, sem)

    def block_of(slot):
        if isinstance(slot, int) and slot == 0:
            return 4
        return jnp.where(slot == 0, 4, lax.rem(my_z + my_y + slot + 1, 4))

    def w_load(slot, third):
        column = third * 1280 + block_of(slot) * 256
        if not isinstance(column, int):
            column = pl.multiple_of(column, 256)
        return load(wqkv_hbm.at[:, pl.ds(column, 256)], wqkv.at[slot * 3 + third], w_sem.at[slot * 3 + third])

    hid_load = load(hidden_hbm, hid, load_sem.at[0])
    mod_load = load(mod_hbm, mod, load_sem.at[1])
    text_load = load(text_hbm, text, load_sem.at[2])
    wout_load = load(wout_hbm, wout, load_sem.at[3])
    wlat_load = load(wlat_hbm, wlat, load_sem.at[4])
    text_load.start()
    hid_load.start()
    mod_load.start()
    for third in range(3):
        w_load(0, third).start()

    barrier = pltpu.get_barrier_semaphore()

    def greet_seq(j, carry):
        pl.semaphore_signal(barrier, inc=1, device_id=(tm, lax.rem(me + j, NSEQ)), device_id_type=MESH)
        return carry

    def greet_tm(j, carry):
        pl.semaphore_signal(barrier, inc=1, device_id=(lax.rem(tm + j, NTM), me), device_id_type=MESH)
        return carry

    lax.fori_loop(1, NSEQ, greet_seq, 0)
    lax.fori_loop(1, NTM, greet_tm, 0)

    def query_rows(device):
        z = device // 4
        place = lax.rem(z + lax.rem(device, 4), 4) * 4 + z
        return pl.ds(pl.multiple_of(place * ROWS, ROWS), ROWS)

    def source_of(kind, to):
        if kind == T:
            return s_t.at[to]
        if kind == KV5:
            return s_kv5.at[extra_item(to)]
        if kind == Q5:
            return s_q5.at[extra_item(to)]
        if kind == QP:
            return s_q.at[to]
        if kind == KVA:
            return s_kva.at[to]
        if kind == KVB:
            return s_kvb.at[to]
        if kind == OP:
            return s_o.at[query_rows(to), :]
        return s_o5.at[pl.ds(pl.multiple_of(to * 64, 64), 64), :]

    def target_of(kind, frm):
        rows = pl.ds(pl.multiple_of(frm * ROWS, ROWS), ROWS)
        if kind == T:
            return r_t.at[:, pl.ds(pl.multiple_of(frm * TROWS, TROWS), TROWS), :]
        if kind == KV5:
            return r_kv5.at[rows, :]
        if kind == Q5:
            return r_q5.at[pl.ds(pl.multiple_of(frm * 64, 64), 64), :]
        if kind == QP:
            return r_q.at[query_rows(frm), :]
        if kind == KVA:
            return r_kva.at[rows, :]
        if kind == KVB:
            return r_kvb.at[rows, :]
        if kind == OP:
            branch, pair = pair_of(frm)
            return mixed.at[pair, pl.ds(pl.multiple_of(branch * ROWS, ROWS), ROWS), :]
        return r_o5.at[extra_item(frm)]

    def transfer(kind, to, frm):
        return pltpu.make_async_remote_copy(
            src_ref=source_of(kind, to),
            dst_ref=target_of(kind, frm),
            send_sem=send_sem.at[kind, to],
            recv_sem=recv_sem.at[kind, frm],
            device_id=(tm, to),
            device_id_type=MESH,
        )

    def keep(kind):
        target_of(kind, me)[...] = source_of(kind, me)[...]

    def send(kind, to):
        @pl.when(to != me)
        def _():
            transfer(kind, to, me).start()

        @pl.when(to == me)
        def _():
            keep(kind)

    def receive_all(kind):
        def one(j, carry):
            frm = lax.rem(me + j, NSEQ)
            pltpu.make_async_remote_copy(
                src_ref=source_of(kind, frm),
                dst_ref=target_of(kind, frm),
                send_sem=send_sem.at[kind, frm],
                recv_sem=recv_sem.at[kind, frm],
                device_id=(tm, frm),
                device_id_type=MESH,
            ).wait_recv()
            return carry

        lax.fori_loop(1, NSEQ, one, 0)

    def sent_slot(slot):
        for z in range(4):
            to = owner(block_of(slot), z)

            @pl.when(to != me)
            def _():
                transfer(QP, to, me).wait_send()
                transfer(KVA, to, me).wait_send()

    def sent_extra():
        for kind in (KV5, Q5):
            for item in range(8):
                to = extra_owner(item)

                @pl.when(to != me)
                def _():
                    transfer(kind, to, me).wait_send()

    def sent_all(kind):
        def one(j, carry):
            transfer(kind, lax.rem(me + j, NSEQ), me).wait_send()
            return carry

        lax.fori_loop(1, NSEQ, one, 0)

    low_row = lax.broadcasted_iota(jnp.int32, (1, 128), 1) < 64
    mean_matrix = head_mean_matrix()
    qg = qgain[...] * (LOG2E / math.sqrt(64))
    qg = jnp.concatenate([qg] * 4, axis=1)
    kg = jnp.concatenate([kgain[...]] * 4, axis=1)

    sig[...] = sigma_of(jnp.full((8, 128), plan[0], jnp.int32).astype(F32))
    text_load.wait()
    for c in range(5):
        lanes = slice(256 * c, 256 * c + 256)
        tk = head_norm(text[:, lanes].astype(F32), kg, mean_matrix)
        tv = text[:, 1280 + 256 * c : 1280 + 256 * c + 256].astype(F32)
        for s in range(2):
            sub = slice(128 * s, 128 * s + 128)
            arrange = keys_first if c == 4 else interleave
            first, second = arrange(tk[:, sub], tv[:, sub], low_row)
            text_kv[4 * c + 2 * s] = first.astype(BF)
            text_kv[4 * c + 2 * s + 1] = second.astype(BF)
    for to in range(NSEQ):
        b, pair = to // 8, 2 * ((to // 4 + to) % 4) + (to // 4) % 2
        s_t[to, 0] = text_kv[2 * pair, TROWS * b : TROWS * b + TROWS]
        s_t[to, 1] = text_kv[2 * pair + 1, TROWS * b : TROWS * b + TROWS]
        item = (to // 4) * 2 + (to % 4) // 2
        b, head = item // 4, 16 + item % 4
        s_t[to, 2] = text_kv[head, TROWS * b : TROWS * b + TROWS]

    hid_load.wait()
    mod_load.wait()

    def first_norm(i, carry):
        rows = pl.ds(pl.multiple_of(i * 32, 32), 32)
        x = normalized(hid[rows, :].astype(F32))
        normed[rows, :] = (x * (1.0 + mod[1]) + mod[0]).astype(BF)
        return carry

    lax.fori_loop(0, 8, first_norm, 0, unroll=4)

    def project(slot):
        parts = []
        for third in range(3):
            w_load(slot, third).wait()
            if isinstance(slot, int):
                for later in (1, 2):
                    w_load(later, third).start()
            part = jnp.dot(normed[...], wqkv[slot * 3 + third], preferred_element_type=F32)
            if third < 2:
                part = part.astype(BF).astype(F32)
                part = head_norm(part, qg if third == 0 else kg, mean_matrix)
            parts.append(part)
        return parts

    q, k, v = project(0)
    for b in range(2):
        for s in range(2):
            lanes = slice(128 * s, 128 * s + 128)
            rows = slice(ROWS * b, ROWS * b + ROWS)
            first, second = keys_first(k[rows, lanes], v[rows, lanes], low_row)
            item = (b * 2 + s) * 2
            s_kv5[item] = first.astype(BF)
            s_kv5[item + 1] = second.astype(BF)
            above = q[ROWS * b : ROWS * b + 64, lanes]
            below = q[ROWS * b + 64 : ROWS * b + ROWS, lanes]
            s_q5[item] = jnp.where(low_row, above, swap(below)).astype(BF)
            s_q5[item + 1] = jnp.where(low_row, swap(above), below).astype(BF)

    for later in (3, 4):
        for third in range(3):
            w_load(later, third).start()
    wout_load.start()
    wlat_load.start()
    pl.semaphore_wait(barrier, NSEQ - 1 + NTM - 1)

    for to in others():
        transfer(T, to, me).start()
    keep(T)
    for to in extra_owners():
        send(KV5, to)
        send(Q5, to)


    def sig_copy(to):
        return pltpu.make_async_remote_copy(
            src_ref=sig, dst_ref=r_sig, send_sem=sig_sem.at[0], recv_sem=sig_sem.at[1],
            device_id=(to, me), device_id_type=MESH,
        )

    @pl.when(tm > 0)
    def _():
        sig_copy(tm - 1).start()

    def whole(slot, carry):
        q, k, v = project(slot)
        block = block_of(slot)
        for b in range(2):
            for s in range(2):
                lanes = slice(128 * s, 128 * s + 128)
                rows = slice(ROWS * b, ROWS * b + ROWS)
                to = owner(block, 2 * b + s)
                first, second = interleave(k[rows, lanes], v[rows, lanes], low_row)
                s_q[to] = q[rows, lanes].astype(BF)
                s_kva[to] = first.astype(BF)
                s_kvb[to] = second.astype(BF)
        @pl.when(slot == 1)
        def _():
            sent_extra()
            sent_all(T)
            receive_all(T)

        for dz in (2, 1, 3, 0):
            to = owner(block, lax.rem(my_z + dz, 4))
            send(QP, to)
            send(KVA, to)
        return carry

    lax.fori_loop(1, 5, whole, 0)

    def bias_of(branch):
        key = lax.broadcasted_iota(jnp.int32, (1, TKEYS), 1)
        return jnp.where(key < lengths[branch], 0.0, NEG_LARGE)

    lane = lax.broadcasted_iota(jnp.int32, (KC, 128), 1)
    low_lanes, high_lanes = lane < 64, lane >= 64
    bias = bias_of(me // 8)
    @pl.when(odd == 0)
    def _():
        receive_all(KV5)
        receive_all(Q5)

        packed = r_q5[...]
        unpacked = jnp.concatenate([packed, swap(packed.astype(F32)).astype(BF)], axis=0)

        def extra_block(i, carry):
            res_a[pl.ds(pl.multiple_of(i * QB, QB), QB), :] = attend(
                r_qx[pl.ds(pl.multiple_of(i * QB, QB), QB), :], r_kv5, r_t.at[2], bias, low_lanes
            )
            return carry

        r_qx[...] = unpacked
        lax.fori_loop(0, 2, extra_block, 0)
        first, second = res_a[0:1024, :], res_a[1024:2048, :]
        above = jnp.where(low_row, swap(first), second)
        below = jnp.where(low_row, first, swap(second))
        s_o5[...] = (above / below).astype(BF)
        for to in others():
            transfer(O5, to, me).start()
        keep(O5)

    for slot in range(1, 4):
        sent_slot(slot)
    for to in others():
        transfer(KVB, to, me).start()
    keep(KVB)

    receive_all(QP)
    receive_all(KVA)

    def first_block(i, carry):
        rows = pl.ds(pl.multiple_of(i * QB, QB), QB)
        res_a[rows, :] = attend(r_q[rows, :], r_kva, r_t.at[0], bias, low_lanes)
        return carry

    lax.fori_loop(0, KEYS // QB, first_block, 0)

    receive_all(KVB)

    def second_block(j, carry):
        start = lax.rem(j + (my_z + my_y + 2) // 2, 2) * QB
        rows = pl.ds(pl.multiple_of(start, QB), QB)
        second = attend(r_q[rows, :], r_kvb, r_t.at[1], bias, high_lanes)
        first = res_a[rows, :]
        above = jnp.where(low_row, second, first)
        below = jnp.where(low_row, first, second)
        s_o[rows, :] = (swap(above) / below).astype(BF)
        for part in range(2):
            for dz in (2, 1, 3, 0):
                send(OP, owner(start // 512 + part, lax.rem(my_z + dz, 4)))
        return carry

    lax.fori_loop(0, KEYS // QB, second_block, 0)

    for item in range(8):
        frm = extra_owner(item)

        @pl.when(frm != me)
        def _():
            transfer(O5, frm, frm).wait_recv()

    for b in range(2):
        for s in range(2):
            item = (b * 2 + s) * 2
            first = r_o5[item].astype(F32)
            second = r_o5[item + 1].astype(F32)
            start = ROWS * b
            mixed[8 + s, start : start + 64, :] = jnp.where(low_row, first, swap(second)).astype(BF)
            mixed[8 + s, start + 64 : start + ROWS, :] = jnp.where(low_row, swap(first), second).astype(BF)
    wout_load.wait()
    wlat_load.wait()

    def add_block(block, first):
        pair = jnp.concatenate([mixed[2 * block], mixed[2 * block + 1]], axis=1)
        depth = pl.ds(pl.multiple_of(block * 256, 256), 256)
        for start in range(0, D, 512):
            stop = min(D, start + 512)
            out = jnp.dot(pair, wout[depth, start:stop], preferred_element_type=F32)
            h2[:, start:stop] = out if first else h2[:, start:stop] + out

    add_block(4, True)
    my_class = lax.rem(my_z + my_y, 4)

    def returned(k, carry):
        block = 2 * lax.rem(my_class // 2 + 1 + k // 2, 2) + lax.rem(k, 2)
        for z in range(4):
            frm = owner(block, z)

            @pl.when(frm != me)
            def _():
                transfer(OP, frm, frm).wait_recv()

        add_block(block, False)
        return carry

    lax.fori_loop(0, 4, returned, 0)

    def second_norm(i, carry):
        rows = pl.ds(pl.multiple_of(i * 32, 32), 32)
        x = normalized(hid[rows, :].astype(F32) + mod[2] * h2[rows, :])
        normed[rows, :] = (x * (1.0 + mod[4]) + mod[3]).astype(BF)
        return carry

    lax.fori_loop(0, 8, second_norm, 0, unroll=4)
    branches = lax.dot_general(wlat[...], normed[...], NT, preferred_element_type=F32)
    guided = guide(branches)
    branches_out[...] = branches

    @pl.when(tm < NTM - 1)
    def _():
        sig_copy(tm).wait_recv()
        next_sig[...] = r_sig[...]

    @pl.when(tm == NTM - 1)
    def _():
        next_sig[...] = jnp.zeros_like(next_sig)

    step = (next_sig[...] - sig[...])[0:1, :]
    drift[...] = step * guided

    def drift_copy(to, frm):
        return pltpu.make_async_remote_copy(
            src_ref=drift, dst_ref=r_drift.at[frm], send_sem=dsend_sem.at[to], recv_sem=drecv_sem.at[frm],
            device_id=(to, me), device_id_type=MESH,
        )

    for to in range(1, NTM):
        @pl.when(to > tm)
        def _():
            drift_copy(to, tm).start()

    total[...] = drift[...]
    for frm in range(NTM - 1):
        @pl.when(frm < tm)
        def _():
            drift_copy(frm, frm).wait_recv()
            total[...] += r_drift[frm]

    for to in range(1, NTM):
        @pl.when(to > tm)
        def _():
            drift_copy(to, tm).wait_send()

    @pl.when(tm > 0)
    def _():
        sig_copy(tm - 1).wait_send()

    for slot in range(4, 5):
        sent_slot(slot)
    for kind in (KVB, OP):
        sent_all(kind)
    @pl.when(odd == 0)
    def _():
        sent_all(O5)


def on_device(
    hidden, text_states, text_lengths, plan_index, modulation, query_key_value_weight, query_gain, key_gain,
    attention_output_weight, latent_output_weight, anchor,
):
    any_spec = pl.BlockSpec(memory_space=pl.ANY)
    vmem = pl.BlockSpec(memory_space=pltpu.VMEM)
    smem = pl.BlockSpec(memory_space=pltpu.SMEM)
    tile = lambda *lead: pltpu.VMEM(lead + (128, 128), BF)
    branches, total = pl.pallas_call(
        kernel,
        out_shape=[jax.ShapeDtypeStruct((64, 2 * ROWS), F32), jax.ShapeDtypeStruct((64, ROWS), F32)],
        in_specs=[any_spec, any_spec, smem, smem, any_spec, any_spec, vmem, vmem, any_spec, any_spec],
        out_specs=[vmem, vmem],
        scratch_shapes=[
            pltpu.VMEM((256, D), BF),
            pltpu.VMEM((32, 2560), BF),
            pltpu.VMEM((5, 1, D), F32),
            pltpu.VMEM((15, D, 256), BF),
            pltpu.VMEM((1280, D), BF),
            pltpu.VMEM((64, D), BF),
            pltpu.VMEM((256, D), BF),
            pltpu.VMEM((256, D), F32),
            pltpu.VMEM((16, 3, TROWS, 128), BF),
            tile(8),
            pltpu.VMEM((8, 64, 128), BF),
            tile(16),
            tile(16),
            tile(16),
            pltpu.VMEM((KEYS, 128), BF),
            pltpu.VMEM((1024, 128), BF),
            pltpu.VMEM((20, 32, 128), BF),
            pltpu.VMEM((3, TKEYS, 128), BF),
            pltpu.VMEM((KEYS, 128), BF),
            pltpu.VMEM((KEYS, 128), BF),
            pltpu.VMEM((1024, 128), BF),
            pltpu.VMEM((KEYS, 128), BF),
            pltpu.VMEM((KEYS, 128), BF),
            pltpu.VMEM((KEYS, 128), BF),
            pltpu.VMEM((8, 64, 128), BF),
            pltpu.VMEM((10, 256, 128), BF),
            pltpu.VMEM((KEYS, 128), F32),
            pltpu.VMEM((64, ROWS), F32),
            pltpu.VMEM((NTM, 64, ROWS), F32),
            pltpu.VMEM((8, 128), F32),
            pltpu.VMEM((8, 128), F32),
            pltpu.VMEM((8, 128), F32),
            pltpu.SemaphoreType.DMA((5,)),
            pltpu.SemaphoreType.DMA((15,)),
            pltpu.SemaphoreType.DMA((8, NSEQ)),
            pltpu.SemaphoreType.DMA((8, NSEQ)),
            pltpu.SemaphoreType.DMA((NTM,)),
            pltpu.SemaphoreType.DMA((NTM,)),
            pltpu.SemaphoreType.DMA((2,)),
        ],
        compiler_params=pltpu.CompilerParams(
            collective_id=0, has_side_effects=True, vmem_limit_bytes=58 * 2**20
        ),
        cost_estimate=pl.CostEstimate(flops=9_600_000_000, bytes_accessed=28_000_000, transcendentals=12_000_000),
    )(
        hidden.reshape(256, D),
        text_states.reshape(32, 2560),
        text_lengths,
        plan_index,
        modulation.transpose(1, 0, 2),
        query_key_value_weight,
        query_gain[None],
        key_gain[None],
        attention_output_weight,
        latent_output_weight.T,
    )
    velocity, latents = pl.pallas_call(
        finish,
        out_shape=[jax.ShapeDtypeStruct((64, ROWS), F32)] * 2,
        in_specs=[vmem] * 3,
        out_specs=[vmem] * 2,
    )(branches, total, anchor.T)
    return velocity.T[None], latents.T[None]


def solution(mesh):
    in_specs = (
        P("tm", None, "seq", None),
        P("tm", None, "seq", None),
        P(),
        P("tm"),
        P("tm", None, None),
        P(),
        P(),
        P(),
        P(),
        P(),
        P("seq", None),
    )
    out_specs = (P("tm", "seq", None), P("tm", "seq", None))
    return jax.shard_map(
        on_device, mesh=mesh, in_specs=in_specs, out_specs=out_specs, check_vma=False
    )
```
